32 devices in a mesh: groups: 2 (over x), blk: 16 (over z, y, core).
Axes of the slice: x: 2, y: 2, z: 4, core: 2. Of those that a mesh axis runs over, the one named last changes fastest.
Arguments:
- queries: bfloat16 [4096, 512], P(('groups', 'blk')), parts along dimension 0, may hold values from -8 to 8
- key_states: bfloat16 [4096, 128], P(('groups', 'blk')), parts along dimension 0, may hold values from -6 to 6
- value_states: bfloat16 [4096, 128], P(('groups', 'blk')), parts along dimension 0, may hold values from -6 to 6
- grad_out: bfloat16 [4096, 512], P(('groups', 'blk')), parts along dimension 0, may hold values from -6 to 6
- tile_mask: int32 [32, 16], P('groups'), parts along dimension 0, may hold values 0 or 1
- block_order: int32 [32], P('groups'), parts along dimension 0, may hold values from 0 to 15, each once
Outputs:
- attended: bfloat16 [4096, 512], P(('groups', 'blk')), parts along dimension 0
- grad_queries: bfloat16 [4096, 512], P(('groups', 'blk')), parts along dimension 0
- grad_keys: float32 [4096, 128], P(('groups', 'blk')), parts along dimension 0
- grad_values: float32 [4096, 128], P(('groups', 'blk')), parts along dimension 0
The draws below stay inside these ranges and needn't reach their ends.
There are 2 independent parts, one for each index of `groups`. The reference program is written for one: setup_inputs(seed, part) draws one part's arguments, and reference() takes and returns one part's arrays. A program takes and returns all parts, laid end to end along the dimension named above; each array names one. Nothing has to cross between parts.
Inputs may be any that keep to these rules, and one draw needn't show every extreme that they name: `block_order`: each block number appears once.
All inputs are finite; a program needn't handle non-finite values.
Results may differ from the reference program's by a relative error of at most 0.04.
Values may be sent and summed in bfloat16 or wider, within the bound.
A program may use at most 64 MiB of HBM per device.

```python
import jax
import jax.numpy as jnp
from jax import lax

HD = 128
HEADS = 4
TILE = 128
TOK_DEV = 128
BLOCKS = 16
SEQ = 2048
NT = 16


def draw_queries(key, part):
    result = jnp.clip(jax.random.normal(jax.random.fold_in(key, 1), (SEQ, HEADS * HD), jnp.float32), -4.0, 4.0)
    return result.astype(jnp.bfloat16)


def draw_key_states(key, part):
    result = jnp.clip(jax.random.normal(jax.random.fold_in(key, 2), (SEQ, HD), jnp.float32), -4.0, 4.0)
    return result.astype(jnp.bfloat16)


def with_ends(array, rng, smallest, largest):
    index_at = [jax.random.randint(jax.random.fold_in(rng, axis), (), 0, length) for axis, length in enumerate(array.shape)]
    widest = array.shape.index(max(array.shape))
    neighbour = index_at[:widest] + [(index_at[widest] + 1) % array.shape[widest]] + index_at[widest + 1:]
    return array.at[tuple(index_at)].set(smallest).at[tuple(neighbour)].set(largest)


def steps_of(stream_key, extent, split, least, top_value):
    def one(position, blocks):
        heights = jax.random.uniform(jax.random.fold_in(jax.random.fold_in(stream_key, 6), position), (blocks,), jnp.float32, least / len(split), top_value / len(split))
        return jnp.repeat(jnp.exp(heights), extent[position] // blocks).reshape((-1,) + (1,) * (len(extent) - position - 1))

    factor_of = one(*split[0])
    for cut in split[1:]:
        factor_of = factor_of * one(*cut)
    return factor_of


def bell_draw(stream_key, dims, deviation, reach, cuts=(), held_as=jnp.bfloat16):
    level = steps_of(stream_key, dims, cuts, -0.22, 0.18) if cuts else 1.0
    values = jax.random.normal(stream_key, dims, jnp.float32) * deviation * level
    return jnp.minimum(jnp.maximum(values, -reach), reach).astype(held_as)


def setup_inputs(seed: int = 0, part: int = 0) -> dict:
    key_list = jax.random.split(jax.random.key(seed), 7)
    part_keys = jax.random.split(jax.random.fold_in(key_list[6], part), 7)
    queries = draw_queries(jax.random.fold_in(jax.random.fold_in(key_list[6], part), 71), part)
    key_states = draw_key_states(jax.random.fold_in(jax.random.fold_in(key_list[6], part), 71), part)
    value_states = bell_draw(part_keys[2], (SEQ, HD), 1.0, 6.0, ((0, 16),))
    grad_out = bell_draw(part_keys[3], (SEQ, HEADS * HD), 1.0, 6.0, ((0, 16),))
    tile_mask = with_ends((jax.random.randint(part_keys[4], (NT, NT), 0, 2) < 1).astype(jnp.int32), jax.random.fold_in(part_keys[4], 1), 0, 1)
    block_order = jax.random.permutation(part_keys[5], BLOCKS).astype(jnp.int32)
    return dict(queries=queries, key_states=key_states, value_states=value_states, grad_out=grad_out, tile_mask=tile_mask, block_order=block_order)


def token_positions(block_order):
    row_ids = jnp.arange(SEQ, dtype=jnp.int32)
    return (block_order[row_ids // TOK_DEV] * TOK_DEV + row_ids % TOK_DEV).astype(jnp.int32)


def reference(queries, key_states, value_states, grad_out, tile_mask, block_order):
    scaling = HD ** -0.5
    positions = token_positions(block_order)
    key_tiles = positions // TILE
    block_rows = min(512, SEQ)
    block_count = SEQ // block_rows

    def mask_for(start):
        query_pos = lax.dynamic_slice_in_dim(positions, start, block_rows)
        query_tiles = query_pos // TILE
        tile_bits = tile_mask[query_tiles[:, None], key_tiles[None, :]]
        same_tile = query_tiles[:, None] == key_tiles[None, :]
        return (query_pos[:, None] >= positions[None, :]) & ((tile_bits == 1) | same_tile)

    def forward_block(block_num):
        start = (block_num * block_rows).astype(jnp.int32)
        allowed = mask_for(start)
        query_block = lax.dynamic_slice_in_dim(queries, start, block_rows)
        outputs = []
        sums = []
        for head_num in range(HEADS):
            query_head = query_block[:, head_num * HD:(head_num + 1) * HD]
            scores = jnp.dot(query_head, key_states.T, preferred_element_type=jnp.float32) * scaling
            scores = jnp.where(allowed, scores, -jnp.inf)
            top_score = jnp.max(scores, axis=1)
            log_sum = top_score + jnp.log(jnp.sum(jnp.exp(scores - top_score[:, None]), axis=1))
            weights = jnp.exp(scores - log_sum[:, None]).astype(jnp.bfloat16)
            outputs.append(jnp.dot(weights, value_states, preferred_element_type=jnp.float32))
            sums.append(log_sum)
        return jnp.concatenate(outputs, axis=1).astype(jnp.bfloat16), jnp.stack(sums, axis=1)

    attended, log_sums = lax.map(forward_block, jnp.arange(block_count, dtype=jnp.int32))
    attended = attended.reshape(SEQ, HEADS * HD)
    log_sums = log_sums.reshape(SEQ, HEADS)

    def backward_block(carry_grads, block_num):
        grad_keys, grad_values = carry_grads
        start = (block_num * block_rows).astype(jnp.int32)
        allowed = mask_for(start)
        query_block = lax.dynamic_slice_in_dim(queries, start, block_rows)
        out_block = lax.dynamic_slice_in_dim(attended, start, block_rows)
        cot_block = lax.dynamic_slice_in_dim(grad_out, start, block_rows)
        sum_block = lax.dynamic_slice_in_dim(log_sums, start, block_rows)
        pieces = []
        for head_num in range(HEADS):
            cols = slice(head_num * HD, (head_num + 1) * HD)
            query_head = query_block[:, cols]
            cot_head = cot_block[:, cols]
            row_delta = jnp.sum(cot_head.astype(jnp.float32) * out_block[:, cols].astype(jnp.float32), axis=1)
            scores = jnp.dot(query_head, key_states.T, preferred_element_type=jnp.float32) * scaling
            scores = jnp.where(allowed, scores, -jnp.inf)
            weights = jnp.exp(scores - sum_block[:, head_num][:, None])
            grad_values = grad_values + jnp.dot(weights.astype(jnp.bfloat16).T, cot_head, preferred_element_type=jnp.float32)
            d_prob = jnp.dot(cot_head, value_states.T, preferred_element_type=jnp.float32)
            d_score = (weights * (d_prob - row_delta[:, None])).astype(jnp.bfloat16)
            pieces.append(jnp.dot(d_score, key_states, preferred_element_type=jnp.float32) * scaling)
            grad_keys = grad_keys + jnp.dot(d_score.T, query_head, preferred_element_type=jnp.float32) * scaling
        return (grad_keys, grad_values), jnp.concatenate(pieces, axis=1).astype(jnp.bfloat16)

    zero_grads = (jnp.zeros((SEQ, HD), jnp.float32), jnp.zeros((SEQ, HD), jnp.float32))
    (grad_keys, grad_values), grad_queries = lax.scan(backward_block, zero_grads, jnp.arange(block_count, dtype=jnp.int32))
    grad_queries = grad_queries.reshape(SEQ, HEADS * HD)
    return attended, grad_queries, grad_keys, grad_values
```

```python
import functools
import math

import jax
import jax.numpy as jnp
from jax import lax
from jax.experimental import pallas as pl
from jax.experimental.pallas import tpu as pltpu
from jax.sharding import PartitionSpec as P

MESH = pl.DeviceIdType.MESH
F32 = jnp.float32
BF16 = jnp.bfloat16
MASKED = -1e30


def dot(a, b):
    return jnp.dot(a, b, preferred_element_type=F32)


def kernel(
    n, q_ref, k_ref, v_ref, g_ref, mask_ref, order_ref, att_ref, dq_ref, dk_ref, dv_ref,
    kv, qr, qt, gr, gt, prob, dprob, maxes, acc, send_a, recv_a, send_b, recv_b, send_c, recv_c,
    gz_s, gz_r, gy_s, gy_r, gc_s, gc_r, a_s, a_r, b_s, b_r, c_s, c_r,
):
    m = n // 4
    tok, hd = k_ref.shape
    heads = q_ref.shape[1] // hd
    rows = heads * tok
    scale = hd ** -0.5
    to_exp2 = scale * math.log2(math.e)

    me = lax.axis_index("blk")
    z, y, c = me // 4, (me // 2) % 2, me % 2

    def index(rz, ry, rc):
        zz = lax.rem(z + rz, m)
        yy = 1 - y if ry else y
        cc = 1 - c if rc else c
        return (zz * 2 + yy) * 2 + cc

    def remote(src, dst, s_sem, r_sem, target):
        return pltpu.make_async_remote_copy(
            src_ref=src, dst_ref=dst, send_sem=s_sem, recv_sem=r_sem,
            device_id={"blk": target}, device_id_type=MESH,
        )

    partner, sibling = index(0, 1, 0), index(0, 0, 1)

    def gather_z(g):
        return remote(kv.at[0, 0, 0], kv.at[m - g, 0, 0], gz_s.at[g], gz_r.at[m - g], index(g, 0, 0))

    def gather_y(rz):
        return remote(kv.at[rz, 0, 0], kv.at[rz, 0, 1], gy_s.at[rz], gy_r.at[rz], partner)

    def gather_c(rz, ry):
        return remote(kv.at[rz, 0, ry], kv.at[rz, 1, ry], gc_s.at[rz, ry], gc_r.at[rz, ry], sibling)

    def sum_a(rz):
        return remote(send_a.at[rz], recv_a.at[rz], a_s.at[rz], a_r.at[rz], sibling)

    def sum_b(rz):
        return remote(send_b.at[rz], recv_b.at[rz], b_s.at[rz], b_r.at[rz], partner)

    def sum_c(rz):
        return remote(send_c.at[rz], recv_c.at[rz], c_s.at[rz], c_r.at[rz], index(rz, 0, 0))

    barrier = pltpu.get_barrier_semaphore()
    for other in [index(g, 0, 0) for g in range(1, m)] + [partner, sibling]:
        pl.semaphore_signal(barrier, inc=1, device_id={"blk": other}, device_id_type=MESH)
    kv[0, 0, 0, 0] = k_ref[...]
    kv[0, 0, 0, 1] = v_ref[...]
    pl.semaphore_wait(barrier, m + 1)

    order = sorted(range(1, m), key=lambda r: min(r, m - r))
    gather_y(0).start()
    gather_c(0, 0).start()
    for rz in order:
        gather_z(m - rz).start()

    for h in range(heads):
        cols = slice(h * hd, (h + 1) * hd)
        lanes = slice(h * tok, (h + 1) * tok)
        qr[lanes, :] = q_ref[:, cols]
        gr[lanes, :] = g_ref[:, cols]
        qt[:, lanes] = q_ref[:, cols].T
        gt[:, lanes] = g_ref[:, cols].T

    my_block = order_ref[me]
    key_ids = lax.broadcasted_iota(jnp.int32, (tok, rows), 0)
    row_ids = lax.broadcasted_iota(jnp.int32, (tok, rows), 1) % tok
    causal = jnp.where(row_ids >= key_ids, 0.0, MASKED).astype(F32)

    def bias(rz, rc, ry):
        if rz == 0 and rc == 0 and ry == 0:
            return causal
        block = order_ref[index(rz, ry, rc)]
        seen = (my_block > block) & (mask_ref[my_block, block] == 1)
        return jnp.where(seen, 0.0, MASKED).astype(F32)

    run_max = jnp.full((1, rows), MASKED, F32)
    run_sum = jnp.zeros((1, rows), F32)
    run_out = jnp.zeros((hd, rows), F32)
    parts = [(rc, ry) for rc in range(2) for ry in range(2)]

    def pump_y(rz):
        gather_y(rz).wait_recv()
        gather_c(rz, 1).start()

    def pump_z(rz):
        gather_z(m - rz).wait_recv()
        gather_y(rz).start()
        gather_c(rz, 0).start()

    steps = [0] + order
    pump_y(0)
    for step, rz in enumerate(steps):
        if step + 1 < len(steps):
            pump_z(steps[step + 1])
        gather_c(rz, 0).wait_recv()
        gather_c(rz, 1).wait_recv()
        keys = kv[rz, :, :, 0].reshape(4 * tok, hd)
        values = kv[rz, :, :, 1].reshape(4 * tok, hd)
        scores = dot(keys, qt[...])
        scores = [
            scores[i * tok:(i + 1) * tok] * to_exp2 + bias(rz, rc, ry)
            for i, (rc, ry) in enumerate(parts)
        ]
        dprob[rz] = dot(values, gt[...])
        new_max = run_max
        for s in scores:
            new_max = jnp.maximum(new_max, jnp.max(s, axis=0, keepdims=True))
        factor = jnp.exp2(run_max - new_max)
        run_sum = run_sum * factor
        for i, s in enumerate(scores):
            p = jnp.exp2(s - new_max)
            run_sum = run_sum + jnp.sum(p, axis=0, keepdims=True)
            prob[rz, i * tok:(i + 1) * tok, :] = p.astype(BF16)
        run_out = run_out * factor + dot(values.T, prob[rz])
        run_max = new_max
        maxes[rz] = new_max
        if step + 1 < len(steps):
            pump_y(steps[step + 1])

    inverse = 1.0 / run_sum
    out_t = (run_out * inverse).astype(BF16)
    delta = jnp.sum(gt[...].astype(F32) * out_t.astype(F32), axis=0, keepdims=True)

    def grads(rz):
        factor = jnp.exp2(maxes[rz] - run_max) * inverse
        wide, scored = [], []
        for i in range(4):
            part = slice(i * tok, (i + 1) * tok)
            w = prob[rz, part, :].astype(F32) * factor
            wide.append(w.astype(BF16))
            ds = (w * (dprob[rz, part, :] - delta)).astype(BF16)
            prob[rz, part, :] = ds
            scored.append(ds)
        dv = dot(jnp.concatenate(wide, axis=0), gr[...])
        dk = dot(jnp.concatenate(scored, axis=0), qr[...])
        for i, (rc, ry) in enumerate(parts):
            part = slice(i * tok, (i + 1) * tok)
            if rc:
                send_a[rz, ry, 0] = dk[part].astype(BF16)
                send_a[rz, ry, 1] = dv[part].astype(BF16)
            else:
                acc[rz, ry, 0] = dk[part]
                acc[rz, ry, 1] = dv[part]
        sum_a(rz).start()

    def level_b(rz):
        sum_a(rz).wait_recv()
        send_b[rz] = (acc[rz, 1] + recv_a[rz, 1].astype(F32)).astype(BF16)
        sum_b(rz).start()

    def level_c(rz):
        sum_b(rz).wait_recv()
        total = acc[rz, 0] + recv_a[rz, 0].astype(F32) + recv_b[rz].astype(F32)
        if rz == 0:
            acc[0, 0] = total
        else:
            send_c[rz] = total.astype(BF16)
            sum_c(rz).start()

    back = order[::-1] + [0]
    for step in range(m + 2):
        if step < m:
            grads(back[step])
        if 1 <= step <= m:
            level_b(back[step - 1])
        if 2 <= step:
            level_c(back[step - 2])

    dq_t = jnp.zeros((hd, rows), F32)
    for rz in range(m):
        dq_t = dq_t + dot(kv[rz, :, :, 0].reshape(4 * tok, hd).T, prob[rz])
    dq_t = (dq_t * scale).astype(BF16)
    for h in range(heads):
        cols = slice(h * hd, (h + 1) * hd)
        lanes = slice(h * tok, (h + 1) * tok)
        att_ref[:, cols] = out_t[:, lanes].T
        dq_ref[:, cols] = dq_t[:, lanes].T

    dk, dv = acc[0, 0, 0], acc[0, 0, 1]
    for rz in back[:-1]:
        sum_c(rz).wait_recv()
        dk = dk + recv_c[rz, 0].astype(F32)
        dv = dv + recv_c[rz, 1].astype(F32)
    dk_ref[...] = dk * scale
    dv_ref[...] = dv

    for rz in range(m):
        gather_y(rz).wait_send()
        gather_c(rz, 0).wait_send()
        gather_c(rz, 1).wait_send()
        sum_a(rz).wait_send()
        sum_b(rz).wait_send()
        if rz:
            gather_z(rz).wait_send()
            sum_c(rz).wait_send()


def shards(queries, key_states, value_states, grad_out, tile_mask, block_order):
    n = lax.axis_size("blk")
    m = n // 4
    tok, hd = key_states.shape
    rows = queries.shape[1] // hd * tok
    assert n == 4 * m and tile_mask.shape[1] == n
    vmem = pl.BlockSpec(memory_space=pltpu.VMEM)
    smem = pl.BlockSpec(memory_space=pltpu.SMEM)
    dma = pltpu.SemaphoreType.DMA
    return pl.pallas_call(
        functools.partial(kernel, n),
        out_shape=(
            jax.ShapeDtypeStruct(queries.shape, BF16),
            jax.ShapeDtypeStruct(queries.shape, BF16),
            jax.ShapeDtypeStruct(key_states.shape, F32),
            jax.ShapeDtypeStruct(key_states.shape, F32),
        ),
        in_specs=[vmem] * 4 + [smem] * 2,
        out_specs=(vmem,) * 4,
        scratch_shapes=[
            pltpu.VMEM((m, 2, 2, 2, tok, hd), BF16),
            pltpu.VMEM((rows, hd), BF16),
            pltpu.VMEM((hd, rows), BF16),
            pltpu.VMEM((rows, hd), BF16),
            pltpu.VMEM((hd, rows), BF16),
            pltpu.VMEM((m, 4 * tok, rows), BF16),
            pltpu.VMEM((m, 4 * tok, rows), F32),
            pltpu.VMEM((m, 1, rows), F32),
            pltpu.VMEM((m, 2, 2, tok, hd), F32),
            pltpu.VMEM((m, 2, 2, tok, hd), BF16),
            pltpu.VMEM((m, 2, 2, tok, hd), BF16),
            pltpu.VMEM((m, 2, tok, hd), BF16),
            pltpu.VMEM((m, 2, tok, hd), BF16),
            pltpu.VMEM((m, 2, tok, hd), BF16),
            pltpu.VMEM((m, 2, tok, hd), BF16),
            dma((m,)), dma((m,)), dma((m,)), dma((m,)), dma((m, 2)), dma((m, 2)),
            dma((m,)), dma((m,)), dma((m,)), dma((m,)), dma((m,)), dma((m,)),
        ],
        compiler_params=pltpu.CompilerParams(
            collective_id=0, has_side_effects=True, vmem_limit_bytes=56 * 1024 * 1024
        ),
    )(queries, key_states, value_states, grad_out, tile_mask, block_order)


def solution(mesh):
    both = P(("groups", "blk"), None)
    return jax.shard_map(
        shards,
        mesh=mesh,
        in_specs=(both, both, both, both, P("groups", None), P("groups")),
        out_specs=(both, both, both, both),
        check_vma=False,
    )
```

```python
import functools
import math

import jax
import jax.numpy as jnp
from jax import lax
from jax.experimental import pallas as pl
from jax.experimental.pallas import tpu as pltpu
from jax.sharding import PartitionSpec as P

MESH = pl.DeviceIdType.MESH
F32 = jnp.float32
BF16 = jnp.bfloat16
MASKED = -1e30
VMEM_BYTES = 58 * 1024 * 1024


def dot(a, b):
    return jnp.dot(a, b, preferred_element_type=F32)


def kernel(
    n, q_hbm, k_hbm, v_hbm, g_hbm, mask_ref, order_ref, att_ref, dq_ref, dk_ref, dv_ref,
    q_ref, g_ref, kv, qr, qt, gr, gt, prob, dprob, maxes, acc, send_a, recv_a, send_b, recv_b, send_c, recv_c,
    in_s, gz_s, gz_r, gy_s, gy_r, gc_s, gc_r, a_s, a_r, b_s, b_r, c_s, c_r,
):
    m = n // 4
    tok, hd = k_hbm.shape
    heads = q_hbm.shape[1] // hd
    rows = heads * tok
    scale = hd ** -0.5
    to_exp2 = scale * math.log2(math.e)
    KEY, VALUE = 0, 1

    me = lax.axis_index("blk")
    z, y, c = me // 4, (me // 2) % 2, me % 2

    def index(rz, ry, rc):
        zz = lax.rem(z + rz, m)
        yy = 1 - y if ry else y
        cc = 1 - c if rc else c
        return (zz * 2 + yy) * 2 + cc

    def remote(src, dst, s_sem, r_sem, target):
        return pltpu.make_async_remote_copy(
            src_ref=src, dst_ref=dst, send_sem=s_sem, recv_sem=r_sem,
            device_id={"blk": target}, device_id_type=MESH,
        )

    partner, sibling = index(0, 1, 1), index(0, 0, 1)

    def side(rz, ry):
        return (1 if rz else 0) ^ ry

    def gather_z(t, g):
        return remote(
            kv.at[t, 0, 0, 0], kv.at[t, m - g, 1, 0], gz_s.at[t, g], gz_r.at[t, m - g], index(g, 0, 1)
        )

    def gather_y(t, rz):
        return remote(
            kv.at[t, rz, side(rz, 0), 0], kv.at[t, rz, side(rz, 1), 1], gy_s.at[t, rz], gy_r.at[t, rz], partner
        )

    def gather_c(t, rz, ry):
        near = side(rz, ry)
        return remote(
            kv.at[t, rz, near, ry], kv.at[t, rz, 1 - near, ry], gc_s.at[t, rz, ry], gc_r.at[t, rz, ry], sibling
        )

    def sum_a(t, rz):
        return remote(send_a.at[t, rz], recv_a.at[t, rz], a_s.at[t, rz], a_r.at[t, rz], sibling)

    def sum_b(t, rz):
        return remote(send_b.at[t, rz], recv_b.at[t, rz], b_s.at[t, rz], b_r.at[t, rz], partner)

    def sum_c(t, rz):
        return remote(send_c.at[t, rz], recv_c.at[t, rz], c_s.at[t, rz], c_r.at[t, rz], index(rz, 0, 1))

    barrier = pltpu.get_barrier_semaphore()
    for other in [index(g, 0, 1) for g in range(1, m)] + [partner, sibling]:
        pl.semaphore_signal(barrier, inc=1, device_id={"blk": other}, device_id_type=MESH)
    loads = [
        pltpu.make_async_copy(src, dst, in_s.at[i])
        for i, (src, dst) in enumerate(
            [(k_hbm, kv.at[KEY, 0, 0, 0]), (v_hbm, kv.at[VALUE, 0, 0, 0]), (q_hbm, q_ref), (g_hbm, g_ref)]
        )
    ]
    for load in loads:
        load.start()
    for load in loads:
        load.wait()
    pl.semaphore_wait(barrier, m + 1)

    order = sorted(range(1, m), key=lambda r: min(r, m - r))
    steps = [0] + order
    back = order[::-1] + [0]
    for t in (KEY, VALUE):
        gather_y(t, 0).start()
        for rz in order:
            gather_z(t, m - rz).start()
        gather_c(t, 0, 0).start()

    for h in range(heads):
        cols = slice(h * hd, (h + 1) * hd)
        lanes = slice(h * tok, (h + 1) * tok)
        qr[lanes, :] = q_ref[:, cols]
        gr[lanes, :] = g_ref[:, cols]
        qt[:, lanes] = q_ref[:, cols].T
        gt[:, lanes] = g_ref[:, cols].T

    my_block = order_ref[me]
    key_ids = lax.broadcasted_iota(jnp.int32, (tok, rows), 0)
    row_ids = lax.broadcasted_iota(jnp.int32, (tok, rows), 1) % tok
    causal = jnp.where(row_ids >= key_ids, 0.0, MASKED).astype(F32)

    def bias(rz, rc, ry):
        if rz == 0 and rc == 0 and ry == 0:
            return causal
        block = order_ref[index(rz, ry, rc)]
        seen = (my_block > block) & (mask_ref[my_block, block] == 1)
        return jnp.where(seen, 0.0, MASKED).astype(F32)

    parts = [(rc, ry) for rc in range(2) for ry in range(2)]

    def pump_y(t, rz):
        gather_y(t, rz).wait_recv()
        gather_c(t, rz, 1).start()

    def pump_z(t, rz):
        gather_z(t, m - rz).wait_recv()
        gather_y(t, rz).start()
        gather_c(t, rz, 0).start()

    def landed(t, rz):
        gather_c(t, rz, 0).wait_recv()
        gather_c(t, rz, 1).wait_recv()
        return kv[t, rz].reshape(4 * tok, hd)

    def score(rz, run_max, run_sum):
        scores = dot(landed(KEY, rz), qt[...])
        scores = [
            scores[i * tok:(i + 1) * tok] * to_exp2 + bias(rz, rc, ry)
            for i, (rc, ry) in enumerate(parts)
        ]
        new_max = run_max
        for s in scores:
            new_max = jnp.maximum(new_max, jnp.max(s, axis=0, keepdims=True))
        run_sum = run_sum * jnp.exp2(run_max - new_max)
        for i, s in enumerate(scores):
            p = jnp.exp2(s - new_max)
            run_sum = run_sum + jnp.sum(p, axis=0, keepdims=True)
            prob[rz, i * tok:(i + 1) * tok, :] = p.astype(BF16)
        maxes[rz] = new_max
        return new_max, run_sum

    for rz in order:
        pump_z(KEY, rz)
    pump_y(KEY, 0)
    run_max = jnp.full((1, rows), MASKED, F32)
    run_sum = jnp.zeros((1, rows), F32)
    run_max, run_sum = score(0, run_max, run_sum)
    for rz in order:
        pump_y(KEY, rz)
        pump_z(VALUE, rz)
    pump_y(VALUE, 0)
    for rz in order:
        run_max, run_sum = score(rz, run_max, run_sum)
    inverse = 1.0 / run_sum

    def hand_over(t, rz, grad):
        for i, (rc, ry) in enumerate(parts):
            part = slice(i * tok, (i + 1) * tok)
            if rc != side(rz, ry):
                send_a[t, rz, ry] = grad[part].astype(BF16)
            else:
                acc[t, rz, ry] = grad[part]
        sum_a(t, rz).start()

    def value_grad(rz):
        factor = jnp.exp2(maxes[rz] - run_max) * inverse
        for i in range(4):
            part = slice(i * tok, (i + 1) * tok)
            prob[rz, part, :] = (prob[rz, part, :].astype(F32) * factor).astype(BF16)
        hand_over(VALUE, rz, dot(prob[rz], gr[...]))

    def key_grad(rz, delta):
        for i in range(4):
            part = slice(i * tok, (i + 1) * tok)
            ds = prob[rz, part, :].astype(F32) * (dprob[rz, part, :] - delta)
            prob[rz, part, :] = ds.astype(BF16)
        hand_over(KEY, rz, dot(prob[rz], qr[...]))

    def level_b(t, rz):
        sum_a(t, rz).wait_recv()
        send_b[t, rz] = (acc[t, rz, 1] + recv_a[t, rz, 1].astype(F32)).astype(BF16)
        sum_b(t, rz).start()

    def level_c(t, rz):
        sum_b(t, rz).wait_recv()
        total = acc[t, rz, 0] + recv_a[t, rz, 0].astype(F32) + recv_b[t, rz].astype(F32)
        if rz == 0:
            acc[t, 0, 0] = total
        else:
            send_c[t, rz] = total.astype(BF16)
            sum_c(t, rz).start()

    for step in range(m + 1):
        if step < m:
            value_grad(back[step])
        if step:
            level_b(VALUE, back[step - 1])
    for rz in order:
        pump_y(VALUE, rz)
    out_t = jnp.zeros((hd, rows), F32)
    for step, rz in enumerate(steps):
        values = landed(VALUE, rz)
        dprob[rz] = dot(values, gt[...])
        out_t = out_t + dot(values.T, prob[rz])
        level_c(VALUE, back[step])
    out_t = out_t.astype(BF16)
    delta = jnp.sum(gt[...].astype(F32) * out_t.astype(F32), axis=0, keepdims=True)

    for step in range(m + 1):
        if step < m:
            key_grad(back[step], delta)
        if step:
            level_b(KEY, back[step - 1])

    for rz in back:
        level_c(KEY, rz)

    dq_t = jnp.zeros((hd, rows), F32)
    for rz in range(m):
        dq_t = dq_t + dot(kv[KEY, rz].reshape(4 * tok, hd).T, prob[rz])
    dq_t = (dq_t * scale).astype(BF16)
    for h in range(heads):
        cols = slice(h * hd, (h + 1) * hd)
        lanes = slice(h * tok, (h + 1) * tok)
        att_ref[:, cols] = out_t[:, lanes].T
        dq_ref[:, cols] = dq_t[:, lanes].T

    for t, out_ref, by in ((VALUE, dv_ref, 1.0), (KEY, dk_ref, scale)):
        total = acc[t, 0, 0]
        for rz in back[:-1]:
            sum_c(t, rz).wait_recv()
            total = total + recv_c[t, rz].astype(F32)
        out_ref[...] = total * by

    for t in (KEY, VALUE):
        for rz in range(m):
            gather_y(t, rz).wait_send()
            gather_c(t, rz, 0).wait_send()
            gather_c(t, rz, 1).wait_send()
            sum_a(t, rz).wait_send()
            sum_b(t, rz).wait_send()
            if rz:
                gather_z(t, rz).wait_send()
                sum_c(t, rz).wait_send()


def write_out(*refs):
    ins, outs, held, in_s, out_s = refs[:4], refs[4:8], refs[8:12], refs[12], refs[13]
    loads = [pltpu.make_async_copy(ins[i], held[i], in_s.at[i]) for i in range(4)]
    stores = [pltpu.make_async_copy(held[i], outs[i], out_s.at[i]) for i in range(4)]
    for load in loads:
        load.start()
    for load, store in zip(loads, stores):
        load.wait()
        store.start()
    for store in stores:
        store.wait()


def shards(queries, key_states, value_states, grad_out, tile_mask, block_order):
    n = lax.axis_size("blk")
    m = n // 4
    tok, hd = key_states.shape
    rows = queries.shape[1] // hd * tok
    assert n == 4 * m and tile_mask.shape[1] == n
    hbm = pl.BlockSpec(memory_space=pl.ANY)
    vmem = pl.BlockSpec(memory_space=pltpu.VMEM)
    smem = pl.BlockSpec(memory_space=pltpu.SMEM)
    dma = pltpu.SemaphoreType.DMA
    shapes = (
        jax.ShapeDtypeStruct(queries.shape, BF16),
        jax.ShapeDtypeStruct(queries.shape, BF16),
        jax.ShapeDtypeStruct(key_states.shape, F32),
        jax.ShapeDtypeStruct(key_states.shape, F32),
    )
    results = pl.pallas_call(
        functools.partial(kernel, n),
        out_shape=shapes,
        in_specs=[hbm] * 4 + [smem] * 2,
        out_specs=(vmem,) * 4,
        scratch_shapes=[
            pltpu.VMEM(queries.shape, BF16),
            pltpu.VMEM(queries.shape, BF16),
            pltpu.VMEM((2, m, 2, 2, tok, hd), BF16),
            pltpu.VMEM((rows, hd), BF16),
            pltpu.VMEM((hd, rows), BF16),
            pltpu.VMEM((rows, hd), BF16),
            pltpu.VMEM((hd, rows), BF16),
            pltpu.VMEM((m, 4 * tok, rows), BF16),
            pltpu.VMEM((m, 4 * tok, rows), F32),
            pltpu.VMEM((m, 1, rows), F32),
            pltpu.VMEM((2, m, 2, tok, hd), F32),
            pltpu.VMEM((2, m, 2, tok, hd), BF16),
            pltpu.VMEM((2, m, 2, tok, hd), BF16),
            pltpu.VMEM((2, m, tok, hd), BF16),
            pltpu.VMEM((2, m, tok, hd), BF16),
            pltpu.VMEM((2, m, tok, hd), BF16),
            pltpu.VMEM((2, m, tok, hd), BF16),
            dma((4,)), dma((2, m)), dma((2, m)), dma((2, m)), dma((2, m)), dma((2, m, 2)), dma((2, m, 2)),
            dma((2, m)), dma((2, m)), dma((2, m)), dma((2, m)), dma((2, m)), dma((2, m)),
        ],
        compiler_params=pltpu.CompilerParams(
            collective_id=0, has_side_effects=True, vmem_limit_bytes=VMEM_BYTES
        ),
    )(queries, key_states, value_states, grad_out, tile_mask, block_order)
    return pl.pallas_call(
        write_out,
        out_shape=shapes,
        in_specs=[hbm] * 4,
        out_specs=(hbm,) * 4,
        scratch_shapes=[pltpu.VMEM(s.shape, s.dtype) for s in shapes] + [dma((4,)), dma((4,))],
        compiler_params=pltpu.CompilerParams(vmem_limit_bytes=VMEM_BYTES),
    )(*results)


def solution(mesh):
    both = P(("groups", "blk"), None)
    return jax.shard_map(
        shards,
        mesh=mesh,
        in_specs=(both, both, both, both, P("groups", None), P("groups")),
        out_specs=(both, both, both, both),
        check_vma=False,
    )
```

```python
import functools
import math

import jax
import jax.numpy as jnp
from jax import lax
from jax.experimental import pallas as pl
from jax.experimental.pallas import tpu as pltpu
from jax.sharding import PartitionSpec as P

MESH = pl.DeviceIdType.MESH
F32 = jnp.float32
BF16 = jnp.bfloat16
MASKED = -1e30


def dot(a, b):
    return jnp.dot(a, b, preferred_element_type=F32)


def kernel(
    n, q_hbm, k_hbm, v_hbm, g_hbm, mask_hbm, order_hbm, att_ref, dq_ref, dk_ref, dv_ref,
    mask_ref, order_ref, q_ref, g_ref, kv, qr, qt, gr, gt, prob, dprob, maxes, acc, send_a, recv_a, send_b, recv_b, send_c, recv_c,
    in_s, gz_s, gz_r, gy_s, gy_r, gc_s, gc_r, a_s, a_r, b_s, b_r, c_s, c_r,
):
    m = n // 4
    tok, hd = k_hbm.shape
    heads = q_hbm.shape[1] // hd
    rows = heads * tok
    scale = hd ** -0.5
    to_exp2 = scale * math.log2(math.e)
    KEY, VALUE = 0, 1

    me = lax.axis_index("blk")
    z, y, c = me // 4, (me // 2) % 2, me % 2

    def index(rz, ry, rc):
        zz = lax.rem(z + rz, m)
        yy = 1 - y if ry else y
        cc = 1 - c if rc else c
        return (zz * 2 + yy) * 2 + cc

    def remote(src, dst, s_sem, r_sem, target):
        return pltpu.make_async_remote_copy(
            src_ref=src, dst_ref=dst, send_sem=s_sem, recv_sem=r_sem,
            device_id={"blk": target}, device_id_type=MESH,
        )

    partner, sibling = index(0, 1, 1), index(0, 0, 1)

    def side(rz, ry):
        return (1 if rz else 0) ^ ry

    def gather_z(t, g):
        return remote(
            kv.at[t, 0, 0, 0], kv.at[t, m - g, 1, 0], gz_s.at[t, g], gz_r.at[t, m - g], index(g, 0, 1)
        )

    def gather_y(t, rz):
        return remote(
            kv.at[t, rz, side(rz, 0), 0], kv.at[t, rz, side(rz, 1), 1], gy_s.at[t, rz], gy_r.at[t, rz], partner
        )

    def gather_c(t, rz, ry):
        near = side(rz, ry)
        return remote(
            kv.at[t, rz, near, ry], kv.at[t, rz, 1 - near, ry], gc_s.at[t, rz, ry], gc_r.at[t, rz, ry], sibling
        )

    def sum_a(t, rz):
        return remote(send_a.at[t, rz], recv_a.at[t, rz], a_s.at[t, rz], a_r.at[t, rz], sibling)

    def sum_b(t, rz):
        return remote(send_b.at[t, rz], recv_b.at[t, rz], b_s.at[t, rz], b_r.at[t, rz], partner)

    def sum_c(t, rz):
        return remote(send_c.at[t, rz], recv_c.at[t, rz], c_s.at[t, rz], c_r.at[t, rz], index(rz, 0, 1))

    barrier = pltpu.get_barrier_semaphore()
    for other in [index(g, 0, 1) for g in range(1, m)] + [partner, sibling]:
        pl.semaphore_signal(barrier, inc=1, device_id={"blk": other}, device_id_type=MESH)
    loads = [
        pltpu.make_async_copy(src, dst, in_s.at[i])
        for i, (src, dst) in enumerate(
            [(k_hbm, kv.at[KEY, 0, 0, 0]), (v_hbm, kv.at[VALUE, 0, 0, 0]), (q_hbm, q_ref), (g_hbm, g_ref),
             (mask_hbm, mask_ref), (order_hbm, order_ref)]
        )
    ]
    for load in loads:
        load.start()
    for load in loads:
        load.wait()
    pl.semaphore_wait(barrier, m + 1)

    order = sorted(range(1, m), key=lambda r: min(r, m - r))
    steps = [0] + order
    back = order[::-1] + [0]
    for t in (KEY, VALUE):
        gather_y(t, 0).start()
        for rz in order:
            gather_z(t, m - rz).start()
        gather_c(t, 0, 0).start()

    for h in range(heads):
        cols = slice(h * hd, (h + 1) * hd)
        lanes = slice(h * tok, (h + 1) * tok)
        qr[lanes, :] = q_ref[:, cols]
        gr[lanes, :] = g_ref[:, cols]
        qt[:, lanes] = q_ref[:, cols].T
        gt[:, lanes] = g_ref[:, cols].T

    my_block = order_ref[me]
    key_ids = lax.broadcasted_iota(jnp.int32, (tok, rows), 0)
    row_ids = lax.broadcasted_iota(jnp.int32, (tok, rows), 1) % tok
    causal = jnp.where(row_ids >= key_ids, 0.0, MASKED).astype(F32)

    def bias(rz, rc, ry):
        if rz == 0 and rc == 0 and ry == 0:
            return causal
        block = order_ref[index(rz, ry, rc)]
        seen = (my_block > block) & (mask_ref[my_block, block] == 1)
        return jnp.where(seen, 0.0, MASKED).astype(F32)

    parts = [(rc, ry) for rc in range(2) for ry in range(2)]

    def pump_y(t, rz):
        gather_y(t, rz).wait_recv()
        gather_c(t, rz, 1).start()

    def pump_z(t, rz):
        gather_z(t, m - rz).wait_recv()
        gather_y(t, rz).start()
        gather_c(t, rz, 0).start()

    def landed(t, rz):
        gather_c(t, rz, 0).wait_recv()
        gather_c(t, rz, 1).wait_recv()
        return kv[t, rz].reshape(4 * tok, hd)

    def score(rz, run_max, run_sum):
        scores = dot(landed(KEY, rz), qt[...])
        scores = [
            scores[i * tok:(i + 1) * tok] * to_exp2 + bias(rz, rc, ry)
            for i, (rc, ry) in enumerate(parts)
        ]
        new_max = run_max
        for s in scores:
            new_max = jnp.maximum(new_max, jnp.max(s, axis=0, keepdims=True))
        run_sum = run_sum * jnp.exp2(run_max - new_max)
        for i, s in enumerate(scores):
            p = jnp.exp2(s - new_max)
            run_sum = run_sum + jnp.sum(p, axis=0, keepdims=True)
            prob[rz, i * tok:(i + 1) * tok, :] = p.astype(BF16)
        maxes[rz] = new_max
        return new_max, run_sum

    for rz in order:
        pump_z(KEY, rz)
    pump_y(KEY, 0)
    run_max = jnp.full((1, rows), MASKED, F32)
    run_sum = jnp.zeros((1, rows), F32)
    run_max, run_sum = score(0, run_max, run_sum)
    for rz in order:
        pump_y(KEY, rz)
        pump_z(VALUE, rz)
    pump_y(VALUE, 0)
    for rz in order:
        run_max, run_sum = score(rz, run_max, run_sum)
    inverse = 1.0 / run_sum

    def hand_over(t, rz, grad):
        for i, (rc, ry) in enumerate(parts):
            part = slice(i * tok, (i + 1) * tok)
            if rc != side(rz, ry):
                send_a[t, rz, ry] = grad[part].astype(BF16)
            else:
                acc[t, rz, ry] = grad[part]
        sum_a(t, rz).start()

    def value_grad(rz):
        factor = jnp.exp2(maxes[rz] - run_max) * inverse
        for i in range(4):
            part = slice(i * tok, (i + 1) * tok)
            prob[rz, part, :] = (prob[rz, part, :].astype(F32) * factor).astype(BF16)
        hand_over(VALUE, rz, dot(prob[rz], gr[...]))

    def key_grad(rz, delta):
        for i in range(4):
            part = slice(i * tok, (i + 1) * tok)
            ds = prob[rz, part, :].astype(F32) * (dprob[rz, part, :] - delta)
            prob[rz, part, :] = ds.astype(BF16)
        hand_over(KEY, rz, dot(prob[rz], qr[...]))

    def level_b(t, rz):
        sum_a(t, rz).wait_recv()
        send_b[t, rz] = (acc[t, rz, 1] + recv_a[t, rz, 1].astype(F32)).astype(BF16)
        sum_b(t, rz).start()

    def level_c(t, rz):
        sum_b(t, rz).wait_recv()
        total = acc[t, rz, 0] + recv_a[t, rz, 0].astype(F32) + recv_b[t, rz].astype(F32)
        if rz == 0:
            acc[t, 0, 0] = total
        else:
            send_c[t, rz] = total.astype(BF16)
            sum_c(t, rz).start()

    for step in range(m + 1):
        if step < m:
            value_grad(back[step])
        if step:
            level_b(VALUE, back[step - 1])
    for rz in order:
        pump_y(VALUE, rz)
    out_t = jnp.zeros((hd, rows), F32)
    for step, rz in enumerate(steps):
        values = landed(VALUE, rz)
        dprob[rz] = dot(values, gt[...])
        out_t = out_t + dot(values.T, prob[rz])
        level_c(VALUE, back[step])
    out_t = out_t.astype(BF16)
    delta = jnp.sum(gt[...].astype(F32) * out_t.astype(F32), axis=0, keepdims=True)

    for step in range(m + 1):
        if step < m:
            key_grad(back[step], delta)
        if step:
            level_b(KEY, back[step - 1])

    for rz in back:
        level_c(KEY, rz)

    dq_t = jnp.zeros((hd, rows), F32)
    for rz in range(m):
        dq_t = dq_t + dot(kv[KEY, rz].reshape(4 * tok, hd).T, prob[rz])
    dq_t = (dq_t * scale).astype(BF16)
    for h in range(heads):
        cols = slice(h * hd, (h + 1) * hd)
        lanes = slice(h * tok, (h + 1) * tok)
        att_ref[:, cols] = out_t[:, lanes].T
        dq_ref[:, cols] = dq_t[:, lanes].T

    for t, out_ref, by in ((VALUE, dv_ref, 1.0), (KEY, dk_ref, scale)):
        total = acc[t, 0, 0]
        for rz in back[:-1]:
            sum_c(t, rz).wait_recv()
            total = total + recv_c[t, rz].astype(F32)
        out_ref[...] = total * by

    for t in (KEY, VALUE):
        for rz in range(m):
            gather_y(t, rz).wait_send()
            gather_c(t, rz, 0).wait_send()
            gather_c(t, rz, 1).wait_send()
            sum_a(t, rz).wait_send()
            sum_b(t, rz).wait_send()
            if rz:
                gather_z(t, rz).wait_send()
                sum_c(t, rz).wait_send()


def write_out(*refs):
    out_s = refs[8]
    stores = [pltpu.make_async_copy(refs[i], refs[4 + i], out_s.at[i]) for i in range(4)]
    for store in stores:
        store.start()
    for store in stores:
        store.wait()


def shards(queries, key_states, value_states, grad_out, tile_mask, block_order):
    n = lax.axis_size("blk")
    m = n // 4
    tok, hd = key_states.shape
    rows = queries.shape[1] // hd * tok
    assert n == 4 * m and tile_mask.shape[1] == n
    hbm = pl.BlockSpec(memory_space=pltpu.HBM)
    vmem = pl.BlockSpec(memory_space=pltpu.VMEM)
    dma = pltpu.SemaphoreType.DMA
    shapes = (
        jax.ShapeDtypeStruct(queries.shape, BF16),
        jax.ShapeDtypeStruct(queries.shape, BF16),
        jax.ShapeDtypeStruct(key_states.shape, F32),
        jax.ShapeDtypeStruct(key_states.shape, F32),
    )
    results = pl.pallas_call(
        functools.partial(kernel, n),
        out_shape=tuple(pltpu.VMEM(s.shape, s.dtype) for s in shapes),
        in_specs=[hbm] * 6,
        out_specs=(vmem,) * 4,
        scratch_shapes=[
            pltpu.SMEM(tile_mask.shape, jnp.int32),
            pltpu.SMEM(block_order.shape, jnp.int32),
            pltpu.VMEM(queries.shape, BF16),
            pltpu.VMEM(queries.shape, BF16),
            pltpu.VMEM((2, m, 2, 2, tok, hd), BF16),
            pltpu.VMEM((rows, hd), BF16),
            pltpu.VMEM((hd, rows), BF16),
            pltpu.VMEM((rows, hd), BF16),
            pltpu.VMEM((hd, rows), BF16),
            pltpu.VMEM((m, 4 * tok, rows), BF16),
            pltpu.VMEM((m, 4 * tok, rows), F32),
            pltpu.VMEM((m, 1, rows), F32),
            pltpu.VMEM((2, m, 2, tok, hd), F32),
            pltpu.VMEM((2, m, 2, tok, hd), BF16),
            pltpu.VMEM((2, m, 2, tok, hd), BF16),
            pltpu.VMEM((2, m, tok, hd), BF16),
            pltpu.VMEM((2, m, tok, hd), BF16),
            pltpu.VMEM((2, m, tok, hd), BF16),
            pltpu.VMEM((2, m, tok, hd), BF16),
            dma((6,)), dma((2, m)), dma((2, m)), dma((2, m)), dma((2, m)), dma((2, m, 2)), dma((2, m, 2)),
            dma((2, m)), dma((2, m)), dma((2, m)), dma((2, m)), dma((2, m)), dma((2, m)),
        ],
        compiler_params=pltpu.CompilerParams(
            collective_id=0, has_side_effects=True, vmem_limit_bytes=58 * 1024 * 1024
        ),
    )(queries, key_states, value_states, grad_out, tile_mask, block_order)
    return pl.pallas_call(
        write_out,
        out_shape=shapes,
        in_specs=[vmem] * 4,
        out_specs=(hbm,) * 4,
        scratch_shapes=[dma((4,))],
        compiler_params=pltpu.CompilerParams(vmem_limit_bytes=8 * 1024 * 1024),
    )(*results)


def solution(mesh):
    both = P(("groups", "blk"), None)
    return jax.shard_map(
        shards,
        mesh=mesh,
        in_specs=(both, both, both, both, P("groups", None), P("groups")),
        out_specs=(both, both, both, both),
        check_vma=False,
    )
```
